128 devices in a mesh: slot: 32 (over x, y, core), ulysses: 4 (over z).
Axes of the slice: x: 4, y: 4, z: 4, core: 2. Of those that a mesh axis runs over, the one named last changes fastest.
Arguments:
- queries: bfloat16 [32768, 3072], P(('slot', 'ulysses')), may hold values from -6 to 6
- key_states: bfloat16 [32768, 3072], P(('slot', 'ulysses')), may hold values from -6 to 6
- value_states: bfloat16 [32768, 3072], P(('slot', 'ulysses')), may hold values from -3.5 to 3.5
- query_gain: float32 [128], replicated, may hold values from 0.1 to 1.9
- key_gain: float32 [128], replicated, may hold values from 0.1 to 1.9
- level_gate: float32 [16, 3072], replicated, may hold values from 0.3 to 1.5
- levels: int32 [32], replicated, may hold values from 0 to 15
- lengths: int32 [32], replicated, may hold values from 512 to 1024, as said below
- context: int32 [32], replicated, may hold values from 0 to 3, as said below
Outputs:
- gated: bfloat16 [32768, 3072], P(('slot', 'ulysses'))
The draws below stay inside these ranges and needn't reach their ends.
Inputs may be any that keep to these rules, and one draw needn't show every extreme that they name: `lengths`: each group uses at least 512 of its token slots; some group uses all 1024. `context`: group c attends to at most c earlier groups; some group attends to 3.
All inputs are finite; a program needn't handle non-finite values.
Results may differ from the reference program's by a relative error of at most 0.0051.
Values may be sent and summed in bfloat16 or wider, within the bound.
A program may use at most 128 MiB of HBM per device.

```python
import math
import jax
import jax.numpy as jnp
from jax import lax

HEADS = 24
HD = 128
CTX = 3
LEVELS = 16
HW = 3072
ST = 1024
GROUPS = 32
TOKENS = 32768


def draw_value_states(key, part):
    key = jax.random.fold_in(key, 11)
    base_key, noise_key = jax.random.split(key)
    base = jax.random.uniform(base_key, (GROUPS, HW), jnp.float32, -1.2, 1.2)
    noise = jnp.clip(0.5 * jax.random.normal(noise_key, (TOKENS, HW), jnp.float32), -2.0, 2.0)
    values = jnp.repeat(base, ST, axis=0) + noise
    return values.astype(jnp.bfloat16)


def draw_lengths(key, part):
    key = jax.random.fold_in(key, 23)
    first_key, second_key = jax.random.split(key)
    counts = jax.random.randint(first_key, (GROUPS,), ST // 2, ST + 1)
    chosen = jax.random.randint(second_key, (), 0, GROUPS)
    return counts.at[chosen].set(ST).astype(jnp.int32)


def draw_context(key, part):
    key = jax.random.fold_in(key, 37)
    first_key, second_key = jax.random.split(key)
    spans = jax.random.randint(first_key, (GROUPS,), 1, CTX + 1)
    spans = jnp.minimum(spans, jnp.arange(GROUPS, dtype=jnp.int32))
    chosen = jax.random.randint(second_key, (), CTX, GROUPS)
    return spans.at[chosen].set(CTX).astype(jnp.int32)


def touch_ends(drawn, key, least, high):
    longest = drawn.shape.index(max(drawn.shape))
    spots = []
    for shift in (0, 1):
        where = [jax.random.randint(jax.random.fold_in(key, axis), (), 0, length) for axis, length in enumerate(drawn.shape)]
        where[longest] = (where[longest] + shift) % drawn.shape[longest]
        spots.append(tuple(where))
    return drawn.at[spots[0]].set(least).at[spots[1]].set(high)


def shard_levels(key, shape, shards, least, high):
    def one(position, shards_of):
        steps = jax.random.uniform(jax.random.fold_in(jax.random.fold_in(key, 6), position), (shards_of,), jnp.float32, least / len(shards), high / len(shards))
        return jnp.repeat(jnp.exp(steps), shape[position] // shards_of).reshape((-1,) + (1,) * (len(shape) - position - 1))

    loudness = one(*shards[0])
    for cut in shards[1:]:
        loudness = loudness * one(*cut)
    return loudness


def bell_draw(own_key, shape, spread, limit, cuts=(), kind=jnp.bfloat16):
    entries = spread * jax.random.normal(own_key, shape, jnp.float32)
    if cuts:
        entries = entries * shard_levels(own_key, shape, cuts, -0.22, 0.18)
    return jnp.clip(entries, -limit, limit).astype(kind)


def setup_inputs(seed: int = 0) -> dict:
    key_of = jax.random.split(jax.random.key(seed), 10)
    queries = bell_draw(key_of[0], (TOKENS, HW), 1.0, 6.0, ((0, 128),))
    key_states = bell_draw(key_of[1], (TOKENS, HW), 1.0, 6.0, ((0, 128),))
    value_states = draw_value_states(jax.random.fold_in(key_of[9], 71), 0)
    query_gain = jnp.clip(1.0 + 0.18 * jax.random.normal(key_of[3], (HD,), jnp.float32), 0.1, 1.9)
    key_gain = jnp.clip(1.0 + 0.18 * jax.random.normal(key_of[4], (HD,), jnp.float32), 0.1, 1.9)
    level_gate = jnp.clip(jnp.exp(jax.random.uniform(key_of[5], (LEVELS, HW), jnp.float32, math.log(0.3), math.log(1.5))), 0.3, 1.5)
    levels = touch_ends(jax.random.randint(key_of[6], (GROUPS,), 0, LEVELS), jax.random.fold_in(key_of[6], 1), 0, LEVELS - 1).astype(jnp.int32)
    lengths = draw_lengths(jax.random.fold_in(key_of[9], 71), 0)
    context = draw_context(jax.random.fold_in(key_of[9], 71), 0)
    return {"queries": queries, "key_states": key_states, "value_states": value_states, "query_gain": query_gain, "key_gain": key_gain, "level_gate": level_gate, "levels": levels, "lengths": lengths, "context": context}


def head_norm(states, gain):
    full = states.astype(jnp.float32).reshape(states.shape[0], HEADS, HD)
    square = lax.optimization_barrier(jnp.mean(full * full, axis=-1, keepdims=True))
    normed = full * lax.rsqrt(square + 1e-06) * gain
    return normed.reshape(states.shape[0], HEADS * HD).astype(jnp.bfloat16)

def reference(queries, key_states, value_states, query_gain, key_gain, level_gate, levels, lengths, context):
    q_norm = head_norm(queries, query_gain).reshape(GROUPS, ST, HEADS, HD)
    k_norm = head_norm(key_states, key_gain).reshape(GROUPS, ST, HEADS, HD)
    value_grid = value_states.reshape(GROUPS, ST, HEADS, HD)
    key_rows = jnp.arange(ST, dtype=jnp.int32)
    factor = 1.0 / math.sqrt(HD)

    def one_group(group_index):
        query_block = q_norm[group_index].astype(jnp.float32)
        reach = context[group_index]
        weighted = jnp.zeros((HEADS, ST, HD), jnp.float32)
        total = jnp.zeros((HEADS, ST), jnp.float32)
        for offset in range(CTX + 1):
            source = jnp.maximum(group_index - offset, 0).astype(jnp.int32)
            key_block = k_norm[source].astype(jnp.float32)
            value_block = value_grid[source].astype(jnp.float32)
            scores = jnp.einsum('qhd,khd->hqk', query_block, key_block) * factor
            allowed = (offset <= reach) & (key_rows < lengths[source])
            weight = jnp.where(allowed[None, None, :], jnp.exp(scores), 0.0)
            total = total + lax.optimization_barrier(jnp.sum(weight, axis=-1))
            packed = lax.optimization_barrier(weight.astype(jnp.bfloat16)).astype(jnp.float32)
            weighted = weighted + jnp.einsum('hqk,khd->hqd', packed, value_block)
        attended = weighted / total[:, :, None]
        attended = jnp.transpose(attended, (1, 0, 2)).reshape(ST, HEADS * HD)
        attended = jnp.where((key_rows < lengths[group_index])[:, None], attended, 0.0)
        attended = lax.optimization_barrier(attended.astype(jnp.bfloat16)).astype(jnp.float32)
        gate_row = level_gate[levels[group_index]]
        return (gate_row[None, :] * attended).astype(jnp.bfloat16)
    gated = lax.map(one_group, jnp.arange(GROUPS, dtype=jnp.int32))
    return gated.reshape(TOKENS, HEADS * HD)
```

```python
import functools
import math

import jax
import jax.numpy as jnp
from jax import lax
from jax.experimental import pallas as pl
from jax.experimental.pallas import tpu as pltpu
from jax.sharding import PartitionSpec as P

HD = 128
CORES = 2
MESH = pl.DeviceIdType.MESH
FACTOR = math.log2(math.e) / math.sqrt(HD)
F32, BF16 = jnp.float32, jnp.bfloat16


def kernel(
    slots, depth, lengths, context, query_gain, key_gain, q_hbm, k_hbm, v_hbm, out_hbm,
    q_in, k_in, v_in, q_own, k_own, v_own, q_far, local, ahead, part, part_sum, back, back_sum, done,
    load_sem, in_send, in_recv, q_send, q_recv, part_send, part_recv, out_send, out_recv,
):
    slot, z = lax.axis_index("slot"), lax.axis_index("ulysses")
    chip, core = slot // CORES, slot % CORES
    chips = slots // CORES
    heads = q_own.shape[0]
    span = q_own.shape[2]
    rows = span // depth
    mine = z * CORES + core
    partners = depth * CORES
    tile = min(256, span)
    blocks = span // HD

    def chip_at(distance):
        return ((chip + distance + chips) % chips) * CORES + core, z

    def partner(r):
        return chip * CORES + (core + r % CORES) % CORES, (z + r // CORES) % depth

    loads = [
        pltpu.make_async_copy(source, target, load_sem.at[i])
        for i, (source, target) in enumerate(((q_hbm, q_in), (k_hbm, k_in), (v_hbm, v_in)))
    ]
    for load in loads:
        load.start()

    barrier = pltpu.get_barrier_semaphore()
    everyone = [partner(r) for r in range(1, partners)] + [chip_at(d) for d in (-2, -1, 1, 2)]
    for other in everyone:
        pl.semaphore_signal(barrier, inc=1, device_id=other, device_id_type=MESH)

    def group(distance):
        return (chip * CORES + distance) % slots

    for g in range(CORES):
        used = lax.broadcasted_iota(jnp.int32, (span, HD), 0) < lengths[group(g)]
        ones = jnp.where(used, 1.0, 0.0).astype(BF16)
        for j in range(heads):
            v_own[j, g, :, HD:] = ones

    for load in loads:
        load.wait()
    pl.semaphore_wait(barrier, len(everyone))

    def columns(owner, j):
        return pl.ds(pl.multiple_of((owner * heads + j) * HD, HD), HD)

    own_rows = pl.ds(pl.multiple_of(z * rows, rows), rows)

    def normalize(ref, cols, gain):
        full = ref[:, cols].astype(F32)
        square = jnp.mean(full * full, axis=-1, keepdims=True)
        ref[:, cols] = (full * lax.rsqrt(square + 1e-06) * gain[...]).astype(BF16)

    def clip_values(cols):
        place = lax.broadcasted_iota(jnp.int32, (rows, HD), 0) + z * rows
        v_in[:, cols] = jnp.where(place < lengths[slot], v_in[:, cols].astype(F32), 0.0).astype(BF16)

    def landing(which, j):
        if which == 2:
            return v_own.at[j, :, :, pl.ds(0, HD)]
        return (q_own, k_own)[which].at[j]

    def send_in(which, j):
        source = (q_in, k_in, v_in)[which]
        if which == 2:
            target = v_own.at[j, core, own_rows, pl.ds(0, HD)]
        else:
            target = (q_own, k_own)[which].at[j, core, own_rows, :]

        def one(r, carry):
            to_slot, to_z = partner(r)
            cols = columns(to_z * CORES + to_slot % CORES, j)
            if which == 0:
                normalize(source, cols, query_gain)
            elif which == 1:
                normalize(source, cols, key_gain)
            else:
                clip_values(cols)

            @pl.when(r == 0)
            def _():
                pltpu.make_async_copy(source.at[:, cols], target, in_recv.at[which, j]).start()

            @pl.when(r > 0)
            def _():
                pltpu.make_async_remote_copy(
                    src_ref=source.at[:, cols], dst_ref=target,
                    send_sem=in_send.at[which, j], recv_sem=in_recv.at[which, j],
                    device_id=(to_slot, to_z), device_id_type=MESH,
                ).start()

            return carry

        lax.fori_loop(0, partners, one, 0)

    def await_in(which, j):
        here = landing(which, j)
        pltpu.make_async_copy(here, here, in_recv.at[which, j]).wait()

    def query_copy(j, n):
        return pltpu.make_async_remote_copy(
            src_ref=q_own.at[j, n % 2], dst_ref=q_far.at[j, n],
            send_sem=q_send.at[j, n], recv_sem=q_recv.at[j, n],
            device_id=chip_at(-2 if n == 2 else -1), device_id_type=MESH,
        )

    def part_copies(j, n):
        return [
            pltpu.make_async_remote_copy(
                src_ref=source.at[j, n], dst_ref=target.at[j, n],
                send_sem=part_send.at[j, n, i], recv_sem=part_recv.at[j, n, i],
                device_id=chip_at(1), device_id_type=MESH,
            )
            for i, (source, target) in enumerate(((part, back), (part_sum, back_sum)))
        ]

    def attend(queries, j, g):
        scores = lax.dot_general(
            queries, k_own[j, g], (((1,), (1,)), ((), ())), preferred_element_type=F32
        )
        weight = jnp.exp2(scores * FACTOR).astype(BF16)
        return jnp.dot(weight, v_own[j, g], preferred_element_type=F32)

    def allowed(distance, offset):
        return jnp.where(context[group(distance)] >= offset, 1.0, 0.0)

    def tiles(body):
        def one(i, carry):
            body(i, pl.ds(pl.multiple_of(i * tile, tile), tile))
            return carry

        lax.fori_loop(0, span // tile, one, 0)

    diagonal = lax.broadcasted_iota(jnp.int32, (HD, HD), 0) == lax.broadcasted_iota(jnp.int32, (HD, HD), 1)

    def keep_part(j, n, i, here, both, arrived):
        number = both[:, :HD]
        if arrived is not None:
            number = number + back[j, arrived, here, :].astype(F32)
        part[j, n, here, :] = number.astype(BF16)
        for s in range(tile // HD):
            line = pl.ds(i * (tile // HD) + s, 1)
            total = both[s * HD:(s + 1) * HD, HD:]
            total = jnp.sum(jnp.where(diagonal, total, 0.0), axis=0, keepdims=True)
            if arrived is not None:
                total = total + back_sum[j, arrived, line, :]
            part_sum[j, n, line, :] = total

    def send_parts(j, n):
        for copy in part_copies(j, n):
            copy.start()

    def queries_out(j):
        await_in(0, j)
        for n in (2, 0, 1):
            query_copy(j, n).start()

    def own_part(j):
        def body(i, here):
            local[j, 0, here, :] = attend(q_own[j, 0, here, :], j, 0)
            queries = q_own[j, 1, here, :]
            local[j, 1, here, :] = attend(queries, j, 1) + allowed(1, 1) * attend(queries, j, 0)

        tiles(body)

    def part_c(j):
        query_copy(j, 2).wait_recv()

        def body(i, here):
            both = allowed(4, 3) * attend(q_far[j, 2, here, :], j, 1)
            keep_part(j, 2, i, here, both, None)

        tiles(body)
        send_parts(j, 2)

    def part_b(j):
        query_copy(j, 1).wait_recv()

        def body(i, here):
            queries = q_far[j, 1, here, :]
            both = allowed(3, 2) * attend(queries, j, 1) + allowed(3, 3) * attend(queries, j, 0)
            keep_part(j, 1, i, here, both, None)

        tiles(body)
        send_parts(j, 1)

    def part_a_begin(j):
        query_copy(j, 0).wait_recv()

        def body(i, here):
            queries = q_far[j, 0, here, :]
            ahead[here, :] = allowed(2, 1) * attend(queries, j, 1) + allowed(2, 2) * attend(queries, j, 0)

        tiles(body)

    def part_a_end(j):
        for copy in part_copies(j, 2):
            copy.wait_recv()
        tiles(lambda i, here: keep_part(j, 0, i, here, ahead[here, :], 2))
        send_parts(j, 0)

    def finish(j, g):
        for copy in part_copies(j, g):
            copy.wait_recv()
        used = lengths[group(g)]

        def body(i, carry):
            here = pl.ds(pl.multiple_of(i * HD, HD), HD)
            both = local[j, g, here, :]
            number = both[:, :HD] + back[j, g, here, :].astype(F32)
            line = back_sum[j, g, pl.ds(i, 1), :]
            total = both[:, HD:] + jnp.broadcast_to(line, (HD, HD)).T
            place = lax.broadcasted_iota(jnp.int32, (HD, HD), 0) + i * HD
            done[j, g, here, :] = jnp.where(place < used, number / total, 0.0).astype(BF16)
            return carry

        lax.fori_loop(0, blocks, body, 0)
        target = out_hbm.at[:, columns(mine, j)]
        for d in range(depth):
            to_z = (z + d) % depth
            source = done.at[j, g, pl.ds(pl.multiple_of(to_z * rows, rows), rows), :]
            to_slot = chip * CORES + g

            @pl.when((to_slot == slot) & (to_z == z))
            def _():
                pltpu.make_async_copy(source, target, out_recv.at[j]).start()

            @pl.when((to_slot != slot) | (to_z != z))
            def _():
                pltpu.make_async_remote_copy(
                    src_ref=source, dst_ref=target, send_sem=out_send.at[j], recv_sem=out_recv.at[j],
                    device_id=(to_slot, to_z), device_id_type=MESH,
                ).start()

    def keys_in(j):
        await_in(1, j)
        await_in(2, j)

    for j in range(heads):
        for which in range(3):
            send_in(which, j)
    queries_out(0)
    keys_in(0)
    own_part(0)
    part_c(0)
    part_b(0)
    part_a_begin(0)
    for j in range(1, heads):
        queries_out(j)
        part_a_end(j - 1)
        keys_in(j)
        own_part(j)
        part_c(j)
        part_b(j)
        part_a_begin(j)
        finish(j - 1, 1)
        finish(j - 1, 0)
    part_a_end(heads - 1)
    finish(heads - 1, 1)
    finish(heads - 1, 0)

    sent = q_in.at[:, pl.ds(0, (partners - 1) * HD)]
    got = q_in.at[:, pl.ds(0, partners * HD)]
    for j in range(heads):
        pltpu.make_async_copy(got, got, out_recv.at[j]).wait()
        pltpu.make_async_copy(sent, sent, out_send.at[j]).wait()
        for which in range(3):
            pltpu.make_async_copy(sent, sent, in_send.at[which, j]).wait()
        for n in range(3):
            query_copy(j, n).wait_send()
            for copy in part_copies(j, n):
                copy.wait_send()


def attention(slots, depth, lengths, context, query_gain, key_gain, queries, key_states, value_states):
    rows, width = queries.shape
    heads = width // (HD * depth * CORES)
    span = rows * depth
    row = pltpu.VMEM((rows, width), BF16)
    lines = (heads, 3, span // HD, HD)
    dma = pltpu.SemaphoreType.DMA
    return pl.pallas_call(
        functools.partial(kernel, slots, depth),
        out_shape=jax.ShapeDtypeStruct((rows, width), BF16),
        in_specs=[pl.BlockSpec(memory_space=pltpu.SMEM)] * 2
        + [pl.BlockSpec(memory_space=pltpu.VMEM)] * 2
        + [pl.BlockSpec(memory_space=pl.ANY)] * 3,
        out_specs=pl.BlockSpec(memory_space=pl.ANY),
        scratch_shapes=[
            row, row, row,
            pltpu.VMEM((heads, CORES, span, HD), BF16),
            pltpu.VMEM((heads, CORES, span, HD), BF16),
            pltpu.VMEM((heads, CORES, span, 2 * HD), BF16),
            pltpu.VMEM((heads, 3, span, HD), BF16),
            pltpu.VMEM((heads, CORES, span, 2 * HD), F32),
            pltpu.VMEM((span, 2 * HD), F32),
            pltpu.VMEM((heads, 3, span, HD), BF16),
            pltpu.VMEM(lines, F32),
            pltpu.VMEM((heads, 3, span, HD), BF16),
            pltpu.VMEM(lines, F32),
            pltpu.VMEM((heads, CORES, span, HD), BF16),
            dma((3,)), dma((3, heads)), dma((3, heads)), dma((heads, 3)), dma((heads, 3)),
            dma((heads, 3, 2)), dma((heads, 3, 2)), dma((heads,)), dma((heads,)),
        ],
        compiler_params=pltpu.CompilerParams(
            collective_id=0, has_side_effects=True, vmem_limit_bytes=50 * 2**20
        ),
        cost_estimate=pl.CostEstimate(
            flops=32 * heads * span * span * HD, bytes_accessed=8 * rows * width,
            transcendentals=8 * heads * span * span,
        ),
    )(lengths, context, query_gain[None, :], key_gain[None, :], queries, key_states, value_states)


def shards(
    slots, depth, queries, key_states, value_states, query_gain, key_gain, level_gate, levels, lengths, context
):
    attended = attention(
        slots, depth, lengths, context, query_gain, key_gain, queries, key_states, value_states
    )
    level_here = levels[lax.axis_index("slot")]
    gate_row = lax.dynamic_slice_in_dim(level_gate, level_here, 1, 0)
    return (gate_row * attended.astype(F32)).astype(BF16)


def solution(mesh):
    split = P(("slot", "ulysses"), None)
    return jax.shard_map(
        functools.partial(shards, mesh.shape["slot"], mesh.shape["ulysses"]),
        mesh=mesh,
        in_specs=(split, split, split) + (P(),) * 6,
        out_specs=split,
        check_vma=False,
    )
```

```python
import functools
import math

import jax
import jax.numpy as jnp
from jax import lax
from jax.experimental import pallas as pl
from jax.experimental.pallas import tpu as pltpu
from jax.sharding import PartitionSpec as P

HD = 128
CORES = 2
MESH = pl.DeviceIdType.MESH
FACTOR = math.log2(math.e) / math.sqrt(HD)
F32, BF16 = jnp.float32, jnp.bfloat16


def kernel(
    slots, depth, levels_hbm, lengths_hbm, context_hbm, query_gain_hbm, key_gain_hbm, gate_hbm,
    q_hbm, k_hbm, v_hbm, out_hbm,
    levels, lengths, context, query_gain, key_gain, gate, q_in, k_in, v_in, q_own, k_own, v_own, q_far, local, ahead, part, part_sum, back, back_sum, done,
    load_sem, in_send, in_recv, q_send, q_recv, part_send, part_recv, out_send, out_recv,
):
    slot, z = lax.axis_index("slot"), lax.axis_index("ulysses")
    chip, core = slot // CORES, slot % CORES
    chips = slots // CORES
    heads = q_own.shape[0]
    span = q_own.shape[2]
    rows = span // depth
    mine = z * CORES + core
    partners = depth * CORES
    tile = span
    blocks = span // HD

    def chip_at(distance):
        return ((chip + distance + chips) % chips) * CORES + core, z

    def partner(r):
        return chip * CORES + (core + r % CORES) % CORES, (z + r // CORES) % depth

    loads = [
        pltpu.make_async_copy(source, target, load_sem.at[i])
        for i, (source, target) in enumerate((
            (lengths_hbm, lengths), (query_gain_hbm, query_gain), (key_gain_hbm, key_gain),
            (q_hbm, q_in), (k_hbm, k_in), (v_hbm, v_in),
            (context_hbm, context), (levels_hbm, levels), (gate_hbm, gate),
        ))
    ]
    for load in loads:
        load.start()

    barrier = pltpu.get_barrier_semaphore()
    everyone = [partner(r) for r in range(1, partners)] + [chip_at(d) for d in (-2, -1, 1, 2)]
    for other in everyone:
        pl.semaphore_signal(barrier, inc=1, device_id=other, device_id_type=MESH)

    def group(distance):
        return (chip * CORES + distance) % slots

    loads[0].wait()
    for g in range(CORES):
        used = lax.broadcasted_iota(jnp.int32, (span, HD), 0) < lengths[group(g)]
        ones = jnp.where(used, 1.0, 0.0).astype(BF16)
        for j in range(heads):
            v_own[j, g, :, HD:] = ones

    for load in loads[1:]:
        load.wait()
    pl.semaphore_wait(barrier, len(everyone))

    def columns(owner, j):
        return pl.ds(pl.multiple_of((owner * heads + j) * HD, HD), HD)

    own_rows = pl.ds(pl.multiple_of(z * rows, rows), rows)

    def normalize(ref, cols, gain):
        full = ref[:, cols].astype(F32)
        square = jnp.mean(full * full, axis=-1, keepdims=True)
        ref[:, cols] = (full * lax.rsqrt(square + 1e-06) * gain[...]).astype(BF16)

    def clip_values(cols):
        place = lax.broadcasted_iota(jnp.int32, (rows, HD), 0) + z * rows
        v_in[:, cols] = jnp.where(place < lengths[slot], v_in[:, cols].astype(F32), 0.0).astype(BF16)

    def landing(which, j, g):
        if which == 2:
            return v_own.at[j, g, :, pl.ds(0, HD)]
        return (q_own, k_own)[which].at[j, g]

    def send_in(which, j):
        source = (q_in, k_in, v_in)[which]
        if which == 2:
            target = v_own.at[j, core, own_rows, pl.ds(0, HD)]
        else:
            target = (q_own, k_own)[which].at[j, core, own_rows, :]

        def one(r, carry):
            to_slot, to_z = partner(r)
            cols = columns(to_z * CORES + to_slot % CORES, j)
            if which == 0:
                normalize(source, cols, query_gain)
            elif which == 1:
                normalize(source, cols, key_gain)
            else:
                clip_values(cols)

            @pl.when(r == 0)
            def _():
                pltpu.make_async_copy(source.at[:, cols], target, in_recv.at[which, j, core]).start()

            @pl.when(r > 0)
            def _():
                pltpu.make_async_remote_copy(
                    src_ref=source.at[:, cols], dst_ref=target,
                    send_sem=in_send.at[which, j], recv_sem=in_recv.at[which, j, core],
                    device_id=(to_slot, to_z), device_id_type=MESH,
                ).start()

            return carry

        lax.fori_loop(0, partners, one, 0)

    def await_in(which, j, g):
        here = landing(which, j, g)
        pltpu.make_async_copy(here, here, in_recv.at[which, j, g]).wait()

    def query_copy(j, n):
        direct = n == 2 and j == 0
        return pltpu.make_async_remote_copy(
            src_ref=q_far.at[j, 0] if n == 2 and not direct else q_own.at[j, n % 2], dst_ref=q_far.at[j, n],
            send_sem=q_send.at[j, n], recv_sem=q_recv.at[j, n],
            device_id=chip_at(-2 if direct else -1), device_id_type=MESH,
        )

    def part_copies(j, n):
        return [
            pltpu.make_async_remote_copy(
                src_ref=source.at[j, n], dst_ref=target.at[j, n],
                send_sem=part_send.at[j, n, i], recv_sem=part_recv.at[j, n, i],
                device_id=chip_at(1), device_id_type=MESH,
            )
            for i, (source, target) in enumerate(((part, back), (part_sum, back_sum)))
        ]

    def attend(queries, j, g):
        scores = lax.dot_general(
            queries, k_own[j, g], (((1,), (1,)), ((), ())), preferred_element_type=F32
        )
        weight = jnp.exp2(scores * FACTOR).astype(BF16)
        return jnp.dot(weight, v_own[j, g], preferred_element_type=F32)

    def allowed(distance, offset):
        return jnp.where(context[group(distance)] >= offset, 1.0, 0.0)

    def tiles(body):
        def one(i, carry):
            body(i, pl.ds(pl.multiple_of(i * tile, tile), tile))
            return carry

        lax.fori_loop(0, span // tile, one, 0)

    diagonal = lax.broadcasted_iota(jnp.int32, (HD, HD), 0) == lax.broadcasted_iota(jnp.int32, (HD, HD), 1)

    def keep_part(j, n, i, here, both, arrived):
        number = both[:, :HD]
        if arrived is not None:
            number = number + back[j, arrived, here, :].astype(F32)
        part[j, n, here, :] = number.astype(BF16)
        for s in range(tile // HD):
            line = pl.ds(i * (tile // HD) + s, 1)
            total = both[s * HD:(s + 1) * HD, HD:]
            total = jnp.sum(jnp.where(diagonal, total, 0.0), axis=0, keepdims=True)
            if arrived is not None:
                total = total + back_sum[j, arrived, line, :]
            part_sum[j, n, line, :] = total

    def send_parts(j, n):
        for copy in part_copies(j, n):
            copy.start()

    def query_a_out(j):
        await_in(0, j, 0)
        if j == 0:
            query_copy(j, 2).start()
        query_copy(j, 0).start()

    def query_b_out(j):
        await_in(0, j, 1)
        query_copy(j, 1).start()

    def query_on(j):
        query_copy(j, 0).wait_recv()
        if j > 0:
            query_copy(j, 2).start()

    def own_a(j):
        def body(i, here):
            local[j, 0, here, :] = attend(q_own[j, 0, here, :], j, 0)

        tiles(body)

    def own_b(j):
        def body(i, here):
            queries = q_own[j, 1, here, :]
            local[j, 1, here, :] = attend(queries, j, 1) + allowed(1, 1) * attend(queries, j, 0)

        tiles(body)

    def part_c(j):
        query_copy(j, 2).wait_recv()

        def body(i, here):
            both = allowed(4, 3) * attend(q_far[j, 2, here, :], j, 1)
            keep_part(j, 2, i, here, both, None)

        tiles(body)
        send_parts(j, 2)

    def part_b(j):
        query_copy(j, 1).wait_recv()

        def body(i, here):
            queries = q_far[j, 1, here, :]
            both = allowed(3, 2) * attend(queries, j, 1) + allowed(3, 3) * attend(queries, j, 0)
            keep_part(j, 1, i, here, both, None)

        tiles(body)
        send_parts(j, 1)

    def part_a_begin(j):
        def body(i, here):
            queries = q_far[j, 0, here, :]
            ahead[here, :] = allowed(2, 1) * attend(queries, j, 1) + allowed(2, 2) * attend(queries, j, 0)

        tiles(body)

    def part_a_end(j):
        for copy in part_copies(j, 2):
            copy.wait_recv()
        tiles(lambda i, here: keep_part(j, 0, i, here, ahead[here, :], 2))
        send_parts(j, 0)

    def finish(j, g):
        for copy in part_copies(j, g):
            copy.wait_recv()
        used = lengths[group(g)]
        levels_here = lax.broadcasted_iota(jnp.int32, (gate.shape[0], HD), 0) == levels[group(g)]
        gate_row = jnp.sum(jnp.where(levels_here, gate[:, columns(mine, j)], 0.0), axis=0, keepdims=True)

        def body(i, carry):
            here = pl.ds(pl.multiple_of(i * HD, HD), HD)
            both = local[j, g, here, :]
            number = both[:, :HD] + back[j, g, here, :].astype(F32)
            line = back_sum[j, g, pl.ds(i, 1), :]
            total = both[:, HD:] + jnp.broadcast_to(line, (HD, HD)).T
            place = lax.broadcasted_iota(jnp.int32, (HD, HD), 0) + i * HD
            attended = jnp.where(place < used, number / total, 0.0).astype(BF16)
            done[j, g, here, :] = (gate_row * attended.astype(F32)).astype(BF16)
            return carry

        lax.fori_loop(0, blocks, body, 0)
        target = out_hbm.at[:, columns(mine, j)]
        for d in range(depth):
            to_z = (z + d) % depth
            source = done.at[j, g, pl.ds(pl.multiple_of(to_z * rows, rows), rows), :]
            to_slot = chip * CORES + g

            @pl.when((to_slot == slot) & (to_z == z))
            def _():
                pltpu.make_async_copy(source, target, out_recv.at[j]).start()

            @pl.when((to_slot != slot) | (to_z != z))
            def _():
                pltpu.make_async_remote_copy(
                    src_ref=source, dst_ref=target, send_sem=out_send.at[j], recv_sem=out_recv.at[j],
                    device_id=(to_slot, to_z), device_id_type=MESH,
                ).start()

    def keys_in(j, g):
        await_in(1, j, g)
        await_in(2, j, g)

    def heads_in(j):
        @pl.when(core == 0)
        def _():
            for which in (0, 1, 2):
                send_in(which, j)

        @pl.when(core != 0)
        def _():
            for which in (1, 2, 0):
                send_in(which, j)

    last = heads - 1
    for j in range(heads):
        heads_in(j)
        if j == 0:
            query_a_out(0)
    query_on(0)
    for j in range(heads):
        keys_in(j, 1)
        if j > 0:
            query_b_out(j)
        part_c(j)
        if j == 0:
            query_b_out(j)
        keys_in(j, 0)
        if j == last:
            for i in range(last - 1):
                finish(i, 0)
                finish(i, 1)
        part_a_begin(j)
        own_a(j)
        if j < last:
            query_a_out(j + 1)
        part_a_end(j)
        part_b(j)
        if j < last:
            query_on(j + 1)
        own_b(j)
    for j in range(max(last - 1, 0), heads):
        finish(j, 0)
        finish(j, 1)

    sent = q_in.at[:, pl.ds(0, (partners - 1) * HD)]
    got = q_in.at[:, pl.ds(0, partners * HD)]
    for j in range(heads):
        pltpu.make_async_copy(got, got, out_recv.at[j]).wait()
        pltpu.make_async_copy(sent, sent, out_send.at[j]).wait()
        for which in range(3):
            pltpu.make_async_copy(sent, sent, in_send.at[which, j]).wait()
        for n in range(3):
            query_copy(j, n).wait_send()
            for copy in part_copies(j, n):
                copy.wait_send()


def attention(slots, depth, levels, lengths, context, query_gain, key_gain, level_gate, queries, key_states, value_states):
    rows, width = queries.shape
    heads = width // (HD * depth * CORES)
    span = rows * depth
    row = pltpu.VMEM((rows, width), BF16)
    lines = (heads, 3, span // HD, HD)
    dma = pltpu.SemaphoreType.DMA
    return pl.pallas_call(
        functools.partial(kernel, slots, depth),
        out_shape=jax.ShapeDtypeStruct((rows, width), BF16),
        in_specs=[pl.BlockSpec(memory_space=pl.ANY)] * 9,
        out_specs=pl.BlockSpec(memory_space=pl.ANY),
        scratch_shapes=[
            pltpu.SMEM(levels.shape, jnp.int32), pltpu.SMEM(lengths.shape, jnp.int32),
            pltpu.SMEM(context.shape, jnp.int32),
            pltpu.VMEM((1, HD), F32), pltpu.VMEM((1, HD), F32), pltpu.VMEM(level_gate.shape, F32),
            row, row, row,
            pltpu.VMEM((heads, CORES, span, HD), BF16),
            pltpu.VMEM((heads, CORES, span, HD), BF16),
            pltpu.VMEM((heads, CORES, span, 2 * HD), BF16),
            pltpu.VMEM((heads, 3, span, HD), BF16),
            pltpu.VMEM((heads, CORES, span, 2 * HD), F32),
            pltpu.VMEM((span, 2 * HD), F32),
            pltpu.VMEM((heads, 3, span, HD), BF16),
            pltpu.VMEM(lines, F32),
            pltpu.VMEM((heads, 3, span, HD), BF16),
            pltpu.VMEM(lines, F32),
            pltpu.VMEM((heads, CORES, span, HD), BF16),
            dma((9,)), dma((3, heads)), dma((3, heads, CORES)), dma((heads, 3)), dma((heads, 3)),
            dma((heads, 3, 2)), dma((heads, 3, 2)), dma((heads,)), dma((heads,)),
        ],
        compiler_params=pltpu.CompilerParams(
            collective_id=0, has_side_effects=True, vmem_limit_bytes=60 * 2**20
        ),
        cost_estimate=pl.CostEstimate(
            flops=32 * heads * span * span * HD, bytes_accessed=8 * rows * width,
            transcendentals=8 * heads * span * span,
        ),
    )(
        levels, lengths, context, query_gain[None, :], key_gain[None, :], level_gate,
        queries, key_states, value_states,
    )


def shards(
    slots, depth, queries, key_states, value_states, query_gain, key_gain, level_gate, levels, lengths, context
):
    return attention(
        slots, depth, levels, lengths, context, query_gain, key_gain, level_gate,
        queries, key_states, value_states,
    )


def solution(mesh):
    split = P(("slot", "ulysses"), None)
    return jax.shard_map(
        functools.partial(shards, mesh.shape["slot"], mesh.shape["ulysses"]),
        mesh=mesh,
        in_specs=(split, split, split) + (P(),) * 6,
        out_specs=split,
        check_vma=False,
    )
```

```python
import functools
import math

import jax
import jax.numpy as jnp
from jax import lax
from jax.experimental import pallas as pl
from jax.experimental.pallas import tpu as pltpu
from jax.sharding import PartitionSpec as P

HD = 128
CORES = 2
CUTS = 2
MESH = pl.DeviceIdType.MESH
FACTOR = math.log2(math.e) / math.sqrt(HD)
F32, BF16 = jnp.float32, jnp.bfloat16


def kernel(
    slots, depth, levels_hbm, lengths_hbm, context_hbm, query_gain_hbm, key_gain_hbm, gate_hbm,
    q_hbm, k_hbm, v_hbm, out_hbm,
    levels, lengths, context, query_gain, key_gain, gate, q_in, k_in, v_in, q_own, k_own, v_own, q_far, local, ahead, part, part_sum, back, back_sum, done,
    load_sem, in_send, in_recv, q_send, q_recv, part_send, part_recv, out_send, out_recv,
):
    slot, z = lax.axis_index("slot"), lax.axis_index("ulysses")
    chip, core = slot // CORES, slot % CORES
    chips = slots // CORES
    heads = q_own.shape[0]
    span = q_own.shape[2]
    rows = span // depth
    mine = z * CORES + core
    partners = depth * CORES
    cuts = part_sum.shape[2]
    piece = span // cuts

    def chip_at(distance):
        return ((chip + distance + chips) % chips) * CORES + core, z

    def partner(r):
        return chip * CORES + (core + r % CORES) % CORES, (z + r // CORES) % depth

    loads = [
        pltpu.make_async_copy(source, target, load_sem.at[i])
        for i, (source, target) in enumerate((
            (lengths_hbm, lengths), (query_gain_hbm, query_gain), (key_gain_hbm, key_gain),
            (q_hbm, q_in), (k_hbm, k_in), (v_hbm, v_in),
            (context_hbm, context), (levels_hbm, levels), (gate_hbm, gate),
        ))
    ]
    for load in loads:
        load.start()

    barrier = pltpu.get_barrier_semaphore()
    everyone = [partner(r) for r in range(1, partners)] + [chip_at(d) for d in (-2, -1, 1, 2)]
    for other in everyone:
        pl.semaphore_signal(barrier, inc=1, device_id=other, device_id_type=MESH)

    def group(distance):
        return (chip * CORES + distance) % slots

    loads[0].wait()
    for g in range(CORES):
        used = lax.broadcasted_iota(jnp.int32, (span, HD), 0) < lengths[group(g)]
        ones = jnp.where(used, 1.0, 0.0).astype(BF16)
        for j in range(heads):
            v_own[j, g, :, HD:] = ones

    for load in loads[1:]:
        load.wait()
    pl.semaphore_wait(barrier, len(everyone))

    def columns(owner, j):
        return pl.ds(pl.multiple_of((owner * heads + j) * HD, HD), HD)

    own_rows = pl.ds(pl.multiple_of(z * rows, rows), rows)

    def normalize(ref, cols, gain):
        full = ref[:, cols].astype(F32)
        square = jnp.mean(full * full, axis=-1, keepdims=True)
        ref[:, cols] = (full * lax.rsqrt(square + 1e-06) * gain[...]).astype(BF16)

    def clip_values(cols):
        place = lax.broadcasted_iota(jnp.int32, (rows, HD), 0) + z * rows
        v_in[:, cols] = jnp.where(place < lengths[slot], v_in[:, cols].astype(F32), 0.0).astype(BF16)

    def landing(which, j, g):
        if which == 2:
            return v_own.at[j, g, :, pl.ds(0, HD)]
        return (q_own, k_own)[which].at[j, g]

    def send_in(which, j):
        source = (q_in, k_in, v_in)[which]
        if which == 2:
            target = v_own.at[j, core, own_rows, pl.ds(0, HD)]
        else:
            target = (q_own, k_own)[which].at[j, core, own_rows, :]

        def one(r, carry):
            to_slot, to_z = partner(r)
            cols = columns(to_z * CORES + to_slot % CORES, j)
            if which == 0:
                normalize(source, cols, query_gain)
            elif which == 1:
                normalize(source, cols, key_gain)
            else:
                clip_values(cols)

            @pl.when(r == 0)
            def _():
                pltpu.make_async_copy(source.at[:, cols], target, in_recv.at[which, j, core]).start()

            @pl.when(r > 0)
            def _():
                pltpu.make_async_remote_copy(
                    src_ref=source.at[:, cols], dst_ref=target,
                    send_sem=in_send.at[which, j], recv_sem=in_recv.at[which, j, core],
                    device_id=(to_slot, to_z), device_id_type=MESH,
                ).start()

            return carry

        lax.fori_loop(0, partners, one, 0)

    def await_in(which, j, g):
        here = landing(which, j, g)
        pltpu.make_async_copy(here, here, in_recv.at[which, j, g]).wait()

    def rows_of(h):
        return pl.ds(h * piece, piece)

    def query_copy(j, n, h):
        direct = n == 2 and j == 0
        source = q_far.at[j, 0] if n == 2 and not direct else q_own.at[j, n % 2]
        return pltpu.make_async_remote_copy(
            src_ref=source.at[rows_of(h)], dst_ref=q_far.at[j, n, rows_of(h)],
            send_sem=q_send.at[j, n, h], recv_sem=q_recv.at[j, n, h],
            device_id=chip_at(-2 if direct else -1), device_id_type=MESH,
        )

    def part_copies(j, n, h):
        return [
            pltpu.make_async_remote_copy(
                src_ref=source, dst_ref=target,
                send_sem=part_send.at[j, n, h, i], recv_sem=part_recv.at[j, n, h, i],
                device_id=chip_at(1), device_id_type=MESH,
            )
            for i, (source, target) in enumerate((
                (part.at[j, n, rows_of(h)], back.at[j, n, rows_of(h)]),
                (part_sum.at[j, n, h], back_sum.at[j, n, h]),
            ))
        ]

    def attend(queries, j, g):
        scores = lax.dot_general(
            queries, k_own[j, g], (((1,), (1,)), ((), ())), preferred_element_type=F32
        )
        weight = jnp.exp2(scores * FACTOR).astype(BF16)
        return jnp.dot(weight, v_own[j, g], preferred_element_type=F32)

    def allowed(distance, offset):
        return jnp.where(context[group(distance)] >= offset, 1.0, 0.0)

    diagonal = lax.broadcasted_iota(jnp.int32, (HD, HD), 0) == lax.broadcasted_iota(jnp.int32, (HD, HD), 1)

    def send_part(j, n, h, both, arrived):
        number = both[:, :HD]
        if arrived is not None:
            number = number + back[j, arrived, rows_of(h), :].astype(F32)
        part[j, n, rows_of(h), :] = number.astype(BF16)
        for s in range(piece // HD):
            total = both[s * HD:(s + 1) * HD, HD:]
            total = jnp.sum(jnp.where(diagonal, total, 0.0), axis=0, keepdims=True)
            if arrived is not None:
                total = total + back_sum[j, arrived, h, s:s + 1, :]
            part_sum[j, n, h, s:s + 1, :] = total
        for copy in part_copies(j, n, h):
            copy.start()

    def query_a_out(j):
        await_in(0, j, 0)
        for h in range(cuts):
            if j == 0:
                query_copy(j, 2, h).start()
            query_copy(j, 0, h).start()

    def query_b_out(j):
        await_in(0, j, 1)
        for h in range(cuts):
            query_copy(j, 1, h).start()

    def query_on(j):
        for h in range(cuts):
            query_copy(j, 0, h).wait_recv()
            if j > 0:
                query_copy(j, 2, h).start()

    def own_a(j):
        local[j, 0] = attend(q_own[j, 0], j, 0)

    def own_b(j):
        queries = q_own[j, 1]
        local[j, 1] = attend(queries, j, 1) + allowed(1, 1) * attend(queries, j, 0)

    def part_c(j):
        for h in range(cuts):
            query_copy(j, 2, h).wait_recv()
            both = allowed(4, 3) * attend(q_far[j, 2, rows_of(h), :], j, 1)
            send_part(j, 2, h, both, None)

    def part_b(j):
        for h in range(cuts):
            query_copy(j, 1, h).wait_recv()
            queries = q_far[j, 1, rows_of(h), :]
            both = allowed(3, 2) * attend(queries, j, 1) + allowed(3, 3) * attend(queries, j, 0)
            send_part(j, 1, h, both, None)

    def part_a_begin(j):
        queries = q_far[j, 0]
        ahead[...] = allowed(2, 1) * attend(queries, j, 1) + allowed(2, 2) * attend(queries, j, 0)

    def part_a_end(j):
        for h in range(cuts):
            for copy in part_copies(j, 2, h):
                copy.wait_recv()
            send_part(j, 0, h, ahead[rows_of(h), :], 2)

    def finish(j, g):
        levels_here = lax.broadcasted_iota(jnp.int32, (gate.shape[0], HD), 0) == levels[group(g)]
        gate_row = jnp.sum(jnp.where(levels_here, gate[:, columns(mine, j)], 0.0), axis=0, keepdims=True)
        target = out_hbm.at[:, columns(mine, j)]
        to_slot = chip * CORES + g
        for h in range(cuts):
            for copy in part_copies(j, g, h):
                copy.wait_recv()
            for s in range(piece // HD):
                first = h * piece + s * HD
                here = pl.ds(first, HD)
                both = local[j, g, here, :]
                number = both[:, :HD] + back[j, g, here, :].astype(F32)
                total = both[:, HD:] + jnp.broadcast_to(back_sum[j, g, h, s:s + 1, :], (HD, HD)).T
                place = lax.broadcasted_iota(jnp.int32, (HD, HD), 0) + first
                attended = jnp.where(place < lengths[group(g)], number / total, 0.0).astype(BF16)
                done[j, g, here, :] = (gate_row * attended.astype(F32)).astype(BF16)
            for to_z in range(h * depth // cuts, (h + 1) * depth // cuts):
                source = done.at[j, g, pl.ds(to_z * rows, rows), :]

                @pl.when((to_slot == slot) & (to_z == z))
                def _():
                    pltpu.make_async_copy(source, target, out_recv.at[j]).start()

                @pl.when((to_slot != slot) | (to_z != z))
                def _():
                    pltpu.make_async_remote_copy(
                        src_ref=source, dst_ref=target, send_sem=out_send.at[j], recv_sem=out_recv.at[j],
                        device_id=(to_slot, to_z), device_id_type=MESH,
                    ).start()

    def keys_in(j, g):
        await_in(1, j, g)
        await_in(2, j, g)

    def heads_in(j):
        @pl.when(core == 0)
        def _():
            for which in (0, 1, 2):
                send_in(which, j)

        @pl.when(core != 0)
        def _():
            for which in (1, 2, 0):
                send_in(which, j)

    last = heads - 1
    for j in range(heads):
        heads_in(j)
        if j == 0:
            query_a_out(0)
    query_on(0)
    for j in range(heads):
        keys_in(j, 1)
        if j > 0:
            query_b_out(j)
        part_c(j)
        if j == 0:
            query_b_out(j)
        keys_in(j, 0)
        if j == last:
            for i in range(last - 1):
                finish(i, 0)
                finish(i, 1)
        part_a_begin(j)
        own_a(j)
        if j < last:
            query_a_out(j + 1)
        else:
            finish(j - 1, 0)
            finish(j - 1, 1)
        part_a_end(j)
        part_b(j)
        if j < last:
            query_on(j + 1)
        own_b(j)
    finish(last, 0)
    finish(last, 1)

    sent = q_in.at[:, pl.ds(0, (partners - 1) * HD)]
    got = q_in.at[:, pl.ds(0, partners * HD)]
    for j in range(heads):
        pltpu.make_async_copy(got, got, out_recv.at[j]).wait()
        pltpu.make_async_copy(sent, sent, out_send.at[j]).wait()
        for which in range(3):
            pltpu.make_async_copy(sent, sent, in_send.at[which, j]).wait()
        for n in range(3):
            for h in range(cuts):
                query_copy(j, n, h).wait_send()
                for copy in part_copies(j, n, h):
                    copy.wait_send()


def attention(slots, depth, levels, lengths, context, query_gain, key_gain, level_gate, queries, key_states, value_states):
    rows, width = queries.shape
    heads = width // (HD * depth * CORES)
    span = rows * depth
    row = pltpu.VMEM((rows, width), BF16)
    cuts = CUTS
    lines = (heads, 3, cuts, span // cuts // HD, HD)
    dma = pltpu.SemaphoreType.DMA
    return pl.pallas_call(
        functools.partial(kernel, slots, depth),
        out_shape=jax.ShapeDtypeStruct((rows, width), BF16),
        in_specs=[pl.BlockSpec(memory_space=pl.ANY)] * 9,
        out_specs=pl.BlockSpec(memory_space=pl.ANY),
        scratch_shapes=[
            pltpu.SMEM(levels.shape, jnp.int32), pltpu.SMEM(lengths.shape, jnp.int32),
            pltpu.SMEM(context.shape, jnp.int32),
            pltpu.VMEM((1, HD), F32), pltpu.VMEM((1, HD), F32), pltpu.VMEM(level_gate.shape, F32),
            row, row, row,
            pltpu.VMEM((heads, CORES, span, HD), BF16),
            pltpu.VMEM((heads, CORES, span, HD), BF16),
            pltpu.VMEM((heads, CORES, span, 2 * HD), BF16),
            pltpu.VMEM((heads, 3, span, HD), BF16),
            pltpu.VMEM((heads, CORES, span, 2 * HD), F32),
            pltpu.VMEM((span, 2 * HD), F32),
            pltpu.VMEM((heads, 3, span, HD), BF16),
            pltpu.VMEM(lines, F32),
            pltpu.VMEM((heads, 3, span, HD), BF16),
            pltpu.VMEM(lines, F32),
            pltpu.VMEM((heads, CORES, span, HD), BF16),
            dma((9,)), dma((3, heads)), dma((3, heads, CORES)), dma((heads, 3, cuts)), dma((heads, 3, cuts)),
            dma((heads, 3, cuts, 2)), dma((heads, 3, cuts, 2)), dma((heads,)), dma((heads,)),
        ],
        compiler_params=pltpu.CompilerParams(
            collective_id=0, has_side_effects=True, vmem_limit_bytes=60 * 2**20
        ),
        cost_estimate=pl.CostEstimate(
            flops=32 * heads * span * span * HD, bytes_accessed=8 * rows * width,
            transcendentals=8 * heads * span * span,
        ),
    )(
        levels, lengths, context, query_gain[None, :], key_gain[None, :], level_gate,
        queries, key_states, value_states,
    )


def shards(
    slots, depth, queries, key_states, value_states, query_gain, key_gain, level_gate, levels, lengths, context
):
    return attention(
        slots, depth, levels, lengths, context, query_gain, key_gain, level_gate,
        queries, key_states, value_states,
    )


def solution(mesh):
    split = P(("slot", "ulysses"), None)
    return jax.shard_map(
        functools.partial(shards, mesh.shape["slot"], mesh.shape["ulysses"]),
        mesh=mesh,
        in_specs=(split, split, split) + (P(),) * 6,
        out_specs=split,
        check_vma=False,
    )
```

```python
import functools
import math

import jax
import jax.numpy as jnp
from jax import lax
from jax.experimental import pallas as pl
from jax.experimental.pallas import tpu as pltpu
from jax.sharding import PartitionSpec as P

HD = 128
CORES = 2
CUTS = 2
MESH = pl.DeviceIdType.MESH
FACTOR = math.log2(math.e) / math.sqrt(HD)
F32, BF16 = jnp.float32, jnp.bfloat16


def kernel(
    slots, depth, levels_hbm, lengths_hbm, context_hbm, query_gain_hbm, key_gain_hbm, gate_hbm,
    q_hbm, k_hbm, v_hbm, out_hbm,
    levels, lengths, context, query_gain, key_gain, gate, q_in, k_in, v_in, q_own, k_own, v_own, q_far, local, ahead, part, part_sum, back, back_sum, done,
    load_sem, in_send, in_recv, q_send, q_recv, part_send, part_recv, out_send, out_recv,
):
    slot, z = lax.axis_index("slot"), lax.axis_index("ulysses")
    chip, core = slot // CORES, slot % CORES
    chips = slots // CORES
    heads = q_own.shape[0]
    span = q_own.shape[2]
    rows = span // depth
    mine = z * CORES + core
    partners = depth * CORES
    cuts = part_sum.shape[2]
    piece = span // cuts

    def chip_at(distance):
        return ((chip + distance + chips) % chips) * CORES + core, z

    def partner(r):
        return chip * CORES + (core + r % CORES) % CORES, (z + r // CORES) % depth

    loads = [
        pltpu.make_async_copy(source, target, load_sem.at[i])
        for i, (source, target) in enumerate((
            (lengths_hbm, lengths), (query_gain_hbm, query_gain), (key_gain_hbm, key_gain),
            (q_hbm, q_in), (k_hbm, k_in), (v_hbm, v_in),
            (context_hbm, context), (levels_hbm, levels), (gate_hbm, gate),
        ))
    ]
    for load in loads:
        load.start()

    barrier = pltpu.get_barrier_semaphore()
    everyone = [partner(r) for r in range(1, partners)] + [chip_at(d) for d in (-1, 1)]
    for other in everyone:
        pl.semaphore_signal(barrier, inc=1, device_id=other, device_id_type=MESH)

    def group(distance):
        return (chip * CORES + distance) % slots

    loads[0].wait()
    for g in range(CORES):
        used = lax.broadcasted_iota(jnp.int32, (span, HD), 0) < lengths[group(g)]
        ones = jnp.where(used, 1.0, 0.0).astype(BF16)
        for j in range(heads):
            v_own[j, g, :, HD:] = ones

    for load in loads[1:]:
        load.wait()
    pl.semaphore_wait(barrier, len(everyone))

    def columns(owner, j):
        return pl.ds(pl.multiple_of((owner * heads + j) * HD, HD), HD)

    own_rows = pl.ds(pl.multiple_of(z * rows, rows), rows)

    def normalize(ref, cols, gain):
        full = ref[:, cols].astype(F32)
        square = jnp.mean(full * full, axis=-1, keepdims=True)
        ref[:, cols] = (full * lax.rsqrt(square + 1e-06) * gain[...]).astype(BF16)

    def clip_values(cols):
        place = lax.broadcasted_iota(jnp.int32, (rows, HD), 0) + z * rows
        v_in[:, cols] = jnp.where(place < lengths[slot], v_in[:, cols].astype(F32), 0.0).astype(BF16)

    def landing(which, j, g):
        if which == 2:
            return v_own.at[j, g, :, pl.ds(0, HD)]
        return (q_own, k_own)[which].at[j, g]

    def send_in(which, j):
        source = (q_in, k_in, v_in)[which]
        if which == 2:
            target = v_own.at[j, core, own_rows, pl.ds(0, HD)]
        else:
            target = (q_own, k_own)[which].at[j, core, own_rows, :]

        def one(r, carry):
            to_slot, to_z = partner(r)
            cols = columns(to_z * CORES + to_slot % CORES, j)
            if which == 0:
                normalize(source, cols, query_gain)
            elif which == 1:
                normalize(source, cols, key_gain)
            else:
                clip_values(cols)

            @pl.when(r == 0)
            def _():
                pltpu.make_async_copy(source.at[:, cols], target, in_recv.at[which, j, core]).start()

            @pl.when(r > 0)
            def _():
                pltpu.make_async_remote_copy(
                    src_ref=source.at[:, cols], dst_ref=target,
                    send_sem=in_send.at[which, j], recv_sem=in_recv.at[which, j, core],
                    device_id=(to_slot, to_z), device_id_type=MESH,
                ).start()

            return carry

        lax.fori_loop(0, partners, one, 0)

    def await_in(which, j, g):
        here = landing(which, j, g)
        pltpu.make_async_copy(here, here, in_recv.at[which, j, g]).wait()

    asks = {0: chip > 0, 1: chip > 0, 2: (chip > 0) & (chip < chips - 1)}
    serves = {0: chip < chips - 1, 1: chip < chips - 1, 2: chip < chips - 2}
    merges = (chip > 0) & (chip < chips - 1)

    def rows_of(h):
        return pl.ds(h * piece, piece)

    def query_copy(j, n, h):
        source = q_far.at[j, 0] if n == 2 else q_own.at[j, n]
        return pltpu.make_async_remote_copy(
            src_ref=source.at[rows_of(h)], dst_ref=q_far.at[j, n, rows_of(h)],
            send_sem=q_send.at[j, n, h], recv_sem=q_recv.at[j, n, h],
            device_id=chip_at(-1), device_id_type=MESH,
        )

    def part_copies(j, n, h):
        return [
            pltpu.make_async_remote_copy(
                src_ref=source, dst_ref=target,
                send_sem=part_send.at[j, n, h, i], recv_sem=part_recv.at[j, n, h, i],
                device_id=chip_at(1), device_id_type=MESH,
            )
            for i, (source, target) in enumerate((
                (part.at[j, n, rows_of(h)], back.at[j, n, rows_of(h)]),
                (part_sum.at[j, n, h], back_sum.at[j, n, h]),
            ))
        ]

    def attend(queries, j, g):
        scores = lax.dot_general(
            queries, k_own[j, g], (((1,), (1,)), ((), ())), preferred_element_type=F32
        )
        weight = jnp.exp2(scores * FACTOR).astype(BF16)
        return jnp.dot(weight, v_own[j, g], preferred_element_type=F32)

    def allowed(distance, offset):
        return jnp.where(context[group(distance)] >= offset, 1.0, 0.0)

    diagonal = lax.broadcasted_iota(jnp.int32, (HD, HD), 0) == lax.broadcasted_iota(jnp.int32, (HD, HD), 1)

    def send_part(j, n, h, both, arrived):
        number = both[:, :HD]
        if arrived is not None:
            number = number + jnp.where(merges, back[j, arrived, rows_of(h), :].astype(F32), 0.0)
        part[j, n, rows_of(h), :] = number.astype(BF16)
        for s in range(piece // HD):
            total = both[s * HD:(s + 1) * HD, HD:]
            total = jnp.sum(jnp.where(diagonal, total, 0.0), axis=0, keepdims=True)
            if arrived is not None:
                total = total + jnp.where(merges, back_sum[j, arrived, h, s:s + 1, :], 0.0)
            part_sum[j, n, h, s:s + 1, :] = total
        for copy in part_copies(j, n, h):
            copy.start()

    def query_a_out(j):
        await_in(0, j, 0)

        @pl.when(asks[0])
        def _():
            for h in range(cuts):
                query_copy(j, 0, h).start()

    def query_b_out(j):
        await_in(0, j, 1)

        @pl.when(asks[1])
        def _():
            for h in range(cuts):
                query_copy(j, 1, h).start()

    def query_on(j):
        for h in range(cuts):

            @pl.when(serves[0])
            def _():
                query_copy(j, 0, h).wait_recv()

            @pl.when(asks[2])
            def _():
                query_copy(j, 2, h).start()

    def own_a(j):
        local[j, 0] = attend(q_own[j, 0], j, 0)

    def own_b(j):
        queries = q_own[j, 1]
        local[j, 1] = attend(queries, j, 1) + allowed(1, 1) * attend(queries, j, 0)

    def part_c(j):
        @pl.when(serves[2])
        def _():
            for h in range(cuts):
                query_copy(j, 2, h).wait_recv()
                both = allowed(4, 3) * attend(q_far[j, 2, rows_of(h), :], j, 1)
                send_part(j, 2, h, both, None)

    def part_b(j):
        @pl.when(serves[1])
        def _():
            for h in range(cuts):
                query_copy(j, 1, h).wait_recv()
                queries = q_far[j, 1, rows_of(h), :]
                both = allowed(3, 2) * attend(queries, j, 1) + allowed(3, 3) * attend(queries, j, 0)
                send_part(j, 1, h, both, None)

    def part_a_begin(j):
        @pl.when(serves[0])
        def _():
            queries = q_far[j, 0]
            ahead[...] = allowed(2, 1) * attend(queries, j, 1) + allowed(2, 2) * attend(queries, j, 0)

    def part_a_end(j):
        for h in range(cuts):

            @pl.when(merges)
            def _():
                for copy in part_copies(j, 2, h):
                    copy.wait_recv()

            @pl.when(serves[0])
            def _():
                send_part(j, 0, h, ahead[rows_of(h), :], 2)

    def finish(j, g):
        levels_here = lax.broadcasted_iota(jnp.int32, (gate.shape[0], HD), 0) == levels[group(g)]
        gate_row = jnp.sum(jnp.where(levels_here, gate[:, columns(mine, j)], 0.0), axis=0, keepdims=True)
        target = out_hbm.at[:, columns(mine, j)]
        to_slot = chip * CORES + g
        for h in range(cuts):

            @pl.when(chip > 0)
            def _():
                for copy in part_copies(j, g, h):
                    copy.wait_recv()

            for s in range(piece // HD):
                first = h * piece + s * HD
                here = pl.ds(first, HD)
                both = local[j, g, here, :]
                number = both[:, :HD] + jnp.where(chip > 0, back[j, g, here, :].astype(F32), 0.0)
                total = jnp.where(chip > 0, back_sum[j, g, h, s:s + 1, :], 0.0)
                total = both[:, HD:] + jnp.broadcast_to(total, (HD, HD)).T
                place = lax.broadcasted_iota(jnp.int32, (HD, HD), 0) + first
                attended = jnp.where(place < lengths[group(g)], number / total, 0.0).astype(BF16)
                done[j, g, here, :] = (gate_row * attended.astype(F32)).astype(BF16)
            for to_z in range(h * depth // cuts, (h + 1) * depth // cuts):
                source = done.at[j, g, pl.ds(to_z * rows, rows), :]

                @pl.when((to_slot == slot) & (to_z == z))
                def _():
                    pltpu.make_async_copy(source, target, out_recv.at[j]).start()

                @pl.when((to_slot != slot) | (to_z != z))
                def _():
                    pltpu.make_async_remote_copy(
                        src_ref=source, dst_ref=target, send_sem=out_send.at[j], recv_sem=out_recv.at[j],
                        device_id=(to_slot, to_z), device_id_type=MESH,
                    ).start()

    def keys_in(j, g):
        await_in(1, j, g)
        await_in(2, j, g)

    def heads_in(j):
        @pl.when(core == 0)
        def _():
            for which in (0, 1, 2):
                send_in(which, j)

        @pl.when(core != 0)
        def _():
            for which in (1, 2, 0):
                send_in(which, j)

    last = heads - 1
    for j in range(heads):
        heads_in(j)
        if j == 0:
            query_a_out(0)
    query_on(0)
    for j in range(last):
        keys_in(j, 1)
        if j > 0:
            query_b_out(j)
        part_c(j)
        if j == 0:
            query_b_out(j)
        keys_in(j, 0)
        part_a_begin(j)
        query_a_out(j + 1)
        own_a(j)
        part_a_end(j)
        part_b(j)
        query_on(j + 1)
        own_b(j)
    keys_in(last, 1)
    query_b_out(last)
    keys_in(last, 0)
    part_a_begin(last)
    for j in range(last - 1):
        finish(j, 0)
        finish(j, 1)
    own_a(last)
    part_c(last)
    finish(last - 1, 0)
    part_a_end(last)
    finish(last - 1, 1)
    part_b(last)
    own_b(last)
    finish(last, 0)
    finish(last, 1)

    sent = q_in.at[:, pl.ds(0, (partners - 1) * HD)]
    got = q_in.at[:, pl.ds(0, partners * HD)]
    for j in range(heads):
        pltpu.make_async_copy(got, got, out_recv.at[j]).wait()
        pltpu.make_async_copy(sent, sent, out_send.at[j]).wait()
        for which in range(3):
            pltpu.make_async_copy(sent, sent, in_send.at[which, j]).wait()
        for n in range(3):
            for h in range(cuts):

                @pl.when(asks[n])
                def _():
                    query_copy(j, n, h).wait_send()

                @pl.when(serves[n])
                def _():
                    for copy in part_copies(j, n, h):
                        copy.wait_send()


def attention(slots, depth, levels, lengths, context, query_gain, key_gain, level_gate, queries, key_states, value_states):
    rows, width = queries.shape
    heads = width // (HD * depth * CORES)
    span = rows * depth
    row = pltpu.VMEM((rows, width), BF16)
    cuts = CUTS
    lines = (heads, 3, cuts, span // cuts // HD, HD)
    dma = pltpu.SemaphoreType.DMA
    return pl.pallas_call(
        functools.partial(kernel, slots, depth),
        out_shape=jax.ShapeDtypeStruct((rows, width), BF16),
        in_specs=[pl.BlockSpec(memory_space=pl.ANY)] * 9,
        out_specs=pl.BlockSpec(memory_space=pl.ANY),
        scratch_shapes=[
            pltpu.SMEM(levels.shape, jnp.int32), pltpu.SMEM(lengths.shape, jnp.int32),
            pltpu.SMEM(context.shape, jnp.int32),
            pltpu.VMEM((1, HD), F32), pltpu.VMEM((1, HD), F32), pltpu.VMEM(level_gate.shape, F32),
            row, row, row,
            pltpu.VMEM((heads, CORES, span, HD), BF16),
            pltpu.VMEM((heads, CORES, span, HD), BF16),
            pltpu.VMEM((heads, CORES, span, 2 * HD), BF16),
            pltpu.VMEM((heads, 3, span, HD), BF16),
            pltpu.VMEM((heads, CORES, span, 2 * HD), F32),
            pltpu.VMEM((span, 2 * HD), F32),
            pltpu.VMEM((heads, 3, span, HD), BF16),
            pltpu.VMEM(lines, F32),
            pltpu.VMEM((heads, 3, span, HD), BF16),
            pltpu.VMEM(lines, F32),
            pltpu.VMEM((heads, CORES, span, HD), BF16),
            dma((9,)), dma((3, heads)), dma((3, heads, CORES)), dma((heads, 3, cuts)), dma((heads, 3, cuts)),
            dma((heads, 3, cuts, 2)), dma((heads, 3, cuts, 2)), dma((heads,)), dma((heads,)),
        ],
        compiler_params=pltpu.CompilerParams(
            collective_id=0, has_side_effects=True, vmem_limit_bytes=60 * 2**20
        ),
        cost_estimate=pl.CostEstimate(
            flops=32 * heads * span * span * HD, bytes_accessed=8 * rows * width,
            transcendentals=8 * heads * span * span,
        ),
    )(
        levels, lengths, context, query_gain[None, :], key_gain[None, :], level_gate,
        queries, key_states, value_states,
    )


def shards(
    slots, depth, queries, key_states, value_states, query_gain, key_gain, level_gate, levels, lengths, context
):
    return attention(
        slots, depth, levels, lengths, context, query_gain, key_gain, level_gate,
        queries, key_states, value_states,
    )


def solution(mesh):
    split = P(("slot", "ulysses"), None)
    return jax.shard_map(
        functools.partial(shards, mesh.shape["slot"], mesh.shape["ulysses"]),
        mesh=mesh,
        in_specs=(split, split, split) + (P(),) * 6,
        out_specs=split,
        check_vma=False,
    )
```

```python
import functools
import math

import jax
import jax.numpy as jnp
from jax import lax
from jax.experimental import pallas as pl
from jax.experimental.pallas import tpu as pltpu
from jax.sharding import PartitionSpec as P

HD = 128
CORES = 2
CUTS = 2
MESH = pl.DeviceIdType.MESH
FACTOR = math.log2(math.e) / math.sqrt(HD)
F32, BF16 = jnp.float32, jnp.bfloat16


def kernel(
    slots, depth, levels_hbm, lengths_hbm, context_hbm, query_gain_hbm, key_gain_hbm, gate_hbm,
    q_hbm, k_hbm, v_hbm, out_hbm,
    levels, lengths, context, query_gain, key_gain, gate, q_in, k_in, v_in, q_own, k_own, v_own, q_far, local, ahead, part, part_sum, back, back_sum, done,
    load_sem, in_send, in_recv, q_send, q_recv, part_send, part_recv, out_send, out_recv,
):
    slot, z = lax.axis_index("slot"), lax.axis_index("ulysses")
    chip, core = slot // CORES, slot % CORES
    chips = slots // CORES
    heads = q_own.shape[0]
    span = q_own.shape[2]
    rows = span // depth
    mine = z * CORES + core
    partners = depth * CORES
    cuts = part_sum.shape[2]
    piece = span // cuts

    def chip_at(distance):
        return ((chip + distance + chips) % chips) * CORES + core, z

    def partner(r):
        return chip * CORES + (core + r % CORES) % CORES, (z + r // CORES) % depth

    loads = [
        pltpu.make_async_copy(source, target, load_sem.at[i])
        for i, (source, target) in enumerate((
            (lengths_hbm, lengths), (query_gain_hbm, query_gain), (key_gain_hbm, key_gain),
            (q_hbm, q_in), (k_hbm, k_in), (v_hbm, v_in),
            (context_hbm, context), (levels_hbm, levels), (gate_hbm, gate),
        ))
    ]
    for load in loads:
        load.start()

    barrier = pltpu.get_barrier_semaphore()
    everyone = [partner(r) for r in range(1, partners)] + [chip_at(d) for d in (-1, 1)]
    for other in everyone:
        pl.semaphore_signal(barrier, inc=1, device_id=other, device_id_type=MESH)

    def group(distance):
        return (chip * CORES + distance) % slots

    loads[0].wait()
    for g in range(CORES):
        used = lax.broadcasted_iota(jnp.int32, (span, HD), 0) < lengths[group(g)]
        ones = jnp.where(used, 1.0, 0.0).astype(BF16)
        for j in range(heads):
            v_own[j, g, :, HD:] = ones

    for load in loads[1:]:
        load.wait()
    pl.semaphore_wait(barrier, len(everyone))

    def columns(owner, j):
        return pl.ds(pl.multiple_of((owner * heads + j) * HD, HD), HD)

    own_rows = pl.ds(pl.multiple_of(z * rows, rows), rows)

    def normalize(ref, cols, gain):
        full = ref[:, cols].astype(F32)
        square = jnp.mean(full * full, axis=-1, keepdims=True)
        ref[:, cols] = (full * lax.rsqrt(square + 1e-06) * gain[...]).astype(BF16)

    def clip_values(cols):
        place = lax.broadcasted_iota(jnp.int32, (rows, HD), 0) + z * rows
        v_in[:, cols] = jnp.where(place < lengths[slot], v_in[:, cols].astype(F32), 0.0).astype(BF16)

    def landing(which, j, g):
        if which == 2:
            return v_own.at[j, g, :, pl.ds(0, HD)]
        return (q_own, k_own)[which].at[j, g]

    def send_in(which, j):
        source = (q_in, k_in, v_in)[which]
        if which == 2:
            target = v_own.at[j, core, own_rows, pl.ds(0, HD)]
        else:
            target = (q_own, k_own)[which].at[j, core, own_rows, :]

        def one(r, carry):
            to_slot, to_z = partner(r)
            cols = columns(to_z * CORES + to_slot % CORES, j)
            if which == 0:
                normalize(source, cols, query_gain)
            elif which == 1:
                normalize(source, cols, key_gain)
            else:
                clip_values(cols)

            @pl.when(r == 0)
            def _():
                pltpu.make_async_copy(source.at[:, cols], target, in_recv.at[which, j, core]).start()

            @pl.when(r > 0)
            def _():
                pltpu.make_async_remote_copy(
                    src_ref=source.at[:, cols], dst_ref=target,
                    send_sem=in_send.at[which, j], recv_sem=in_recv.at[which, j, core],
                    device_id=(to_slot, to_z), device_id_type=MESH,
                ).start()

            return carry

        lax.fori_loop(0, partners, one, 0)

    def await_in(which, j, g):
        here = landing(which, j, g)
        pltpu.make_async_copy(here, here, in_recv.at[which, j, g]).wait()

    asks = {0: chip > 0, 1: chip > 0, 2: (chip > 0) & (chip < chips - 1)}
    serves = {0: chip < chips - 1, 1: chip < chips - 1, 2: chip < chips - 2}
    merges = (chip > 0) & (chip < chips - 1)

    def rows_of(h):
        return pl.ds(h * piece, piece)

    def query_copy(j, n, h):
        source = q_far.at[j, 0] if n == 2 else q_own.at[j, n]
        return pltpu.make_async_remote_copy(
            src_ref=source.at[rows_of(h)], dst_ref=q_far.at[j, n, rows_of(h)],
            send_sem=q_send.at[j, n, h], recv_sem=q_recv.at[j, n, h],
            device_id=chip_at(-1), device_id_type=MESH,
        )

    def part_copies(j, n, h):
        return [
            pltpu.make_async_remote_copy(
                src_ref=source, dst_ref=target,
                send_sem=part_send.at[j, n, h, i], recv_sem=part_recv.at[j, n, h, i],
                device_id=chip_at(1), device_id_type=MESH,
            )
            for i, (source, target) in enumerate((
                (part.at[j, n, rows_of(h)], back.at[j, n, rows_of(h)]),
                (part_sum.at[j, n, h], back_sum.at[j, n, h]),
            ))
        ]

    def attend(queries, j, g):
        scores = lax.dot_general(
            queries, k_own[j, g], (((1,), (1,)), ((), ())), preferred_element_type=F32
        )
        weight = jnp.exp2(scores * FACTOR).astype(BF16)
        return jnp.dot(weight, v_own[j, g], preferred_element_type=F32)

    def allowed(distance, offset):
        return jnp.where(context[group(distance)] >= offset, 1.0, 0.0)

    diagonal = lax.broadcasted_iota(jnp.int32, (HD, HD), 0) == lax.broadcasted_iota(jnp.int32, (HD, HD), 1)

    def send_part(j, n, h, both, arrived):
        number = both[:, :HD]
        if arrived is not None:
            number = number + jnp.where(merges, back[j, arrived, rows_of(h), :].astype(F32), 0.0)
        part[j, n, rows_of(h), :] = number.astype(BF16)
        for s in range(piece // HD):
            total = both[s * HD:(s + 1) * HD, HD:]
            total = jnp.sum(jnp.where(diagonal, total, 0.0), axis=0, keepdims=True)
            if arrived is not None:
                total = total + jnp.where(merges, back_sum[j, arrived, h, s:s + 1, :], 0.0)
            part_sum[j, n, h, s:s + 1, :] = total
        for copy in part_copies(j, n, h):
            copy.start()

    def query_a_out(j):
        await_in(0, j, 0)

        @pl.when(asks[0])
        def _():
            for h in range(cuts):
                query_copy(j, 0, h).start()

    def query_b_out(j):
        await_in(0, j, 1)

        @pl.when(asks[1])
        def _():
            for h in range(cuts):
                query_copy(j, 1, h).start()

    def query_on(j):
        for h in range(cuts):

            @pl.when(serves[0])
            def _():
                query_copy(j, 0, h).wait_recv()

            @pl.when(asks[2])
            def _():
                query_copy(j, 2, h).start()

    def own_a(j):
        local[j, 0] = attend(q_own[j, 0], j, 0)

    def own_b(j):
        queries = q_own[j, 1]
        local[j, 1] = attend(queries, j, 1) + allowed(1, 1) * attend(queries, j, 0)

    def part_c(j):
        @pl.when(serves[2])
        def _():
            for h in range(cuts):
                query_copy(j, 2, h).wait_recv()
                both = allowed(4, 3) * attend(q_far[j, 2, rows_of(h), :], j, 1)
                send_part(j, 2, h, both, None)

    def part_b(j):
        @pl.when(serves[1])
        def _():
            for h in range(cuts):
                query_copy(j, 1, h).wait_recv()
                queries = q_far[j, 1, rows_of(h), :]
                both = allowed(3, 2) * attend(queries, j, 1) + allowed(3, 3) * attend(queries, j, 0)
                send_part(j, 1, h, both, None)

    def part_a_begin(j):
        @pl.when(serves[0])
        def _():
            queries = q_far[j, 0]
            ahead[...] = allowed(2, 1) * attend(queries, j, 1) + allowed(2, 2) * attend(queries, j, 0)

    def part_a_end(j):
        for h in range(cuts):

            @pl.when(merges)
            def _():
                for copy in part_copies(j, 2, h):
                    copy.wait_recv()

            @pl.when(serves[0])
            def _():
                send_part(j, 0, h, ahead[rows_of(h), :], 2)

    def finish(j, g):
        levels_here = lax.broadcasted_iota(jnp.int32, (gate.shape[0], HD), 0) == levels[group(g)]
        gate_row = jnp.sum(jnp.where(levels_here, gate[:, columns(mine, j)], 0.0), axis=0, keepdims=True)
        target = out_hbm.at[:, columns(mine, j)]
        to_slot = chip * CORES + g
        for h in range(cuts):

            @pl.when(chip > 0)
            def _():
                for copy in part_copies(j, g, h):
                    copy.wait_recv()

            for s in range(piece // HD):
                first = h * piece + s * HD
                here = pl.ds(first, HD)
                both = local[j, g, here, :]
                number = both[:, :HD] + jnp.where(chip > 0, back[j, g, here, :].astype(F32), 0.0)
                total = jnp.where(chip > 0, back_sum[j, g, h, s:s + 1, :], 0.0)
                total = both[:, HD:] + jnp.broadcast_to(total, (HD, HD)).T
                place = lax.broadcasted_iota(jnp.int32, (HD, HD), 0) + first
                attended = jnp.where(place < lengths[group(g)], number / total, 0.0).astype(BF16)
                done[j, g, here, :] = (gate_row * attended.astype(F32)).astype(BF16)
            for to_z in range(h * depth // cuts, (h + 1) * depth // cuts):
                source = done.at[j, g, pl.ds(to_z * rows, rows), :]

                @pl.when((to_slot == slot) & (to_z == z))
                def _():
                    pltpu.make_async_copy(source, target, out_recv.at[j]).start()

                @pl.when((to_slot != slot) | (to_z != z))
                def _():
                    pltpu.make_async_remote_copy(
                        src_ref=source, dst_ref=target, send_sem=out_send.at[j], recv_sem=out_recv.at[j],
                        device_id=(to_slot, to_z), device_id_type=MESH,
                    ).start()

    def keys_in(j, g):
        await_in(1, j, g)
        await_in(2, j, g)

    def heads_in(j):
        @pl.when(core == 0)
        def _():
            for which in (0, 1, 2):
                send_in(which, j)

        @pl.when(core != 0)
        def _():
            for which in (1, 2, 0):
                send_in(which, j)

    last = heads - 1
    for j in range(heads):
        heads_in(j)
        if j == 0:
            query_a_out(0)
    query_on(0)
    for j in range(last):
        keys_in(j, 1)
        if j > 0:
            query_b_out(j)
        part_c(j)
        if j == 0:
            query_b_out(j)
        keys_in(j, 0)
        part_a_begin(j)
        query_a_out(j + 1)
        own_a(j)
        part_a_end(j)
        part_b(j)
        query_on(j + 1)
        own_b(j)
    keys_in(last, 1)
    query_b_out(last)
    keys_in(last, 0)
    part_a_begin(last)
    for j in range(last - 1):
        finish(j, 0)
        finish(j, 1)
    own_a(last)
    part_c(last)
    finish(last - 1, 0)
    part_a_end(last)
    finish(last - 1, 1)
    part_b(last)
    own_b(last)
    finish(last, 0)
    finish(last, 1)

    sent = q_in.at[:, pl.ds(0, (partners - 1) * HD)]
    got = q_in.at[:, pl.ds(0, partners * HD)]
    for j in range(heads):
        pltpu.make_async_copy(got, got, out_recv.at[j]).wait()
        pltpu.make_async_copy(sent, sent, out_send.at[j]).wait()
        for which in range(3):
            pltpu.make_async_copy(sent, sent, in_send.at[which, j]).wait()
        for n in range(3):
            for h in range(cuts):

                @pl.when(asks[n])
                def _():
                    query_copy(j, n, h).wait_send()

                @pl.when(serves[n])
                def _():
                    for copy in part_copies(j, n, h):
                        copy.wait_send()


def attention(slots, depth, levels, lengths, context, query_gain, key_gain, level_gate, queries, key_states, value_states):
    rows, width = queries.shape
    heads = width // (HD * depth * CORES)
    span = rows * depth
    row = pltpu.VMEM((rows, width), BF16)
    cuts = CUTS
    lines = (heads, 3, cuts, span // cuts // HD, HD)
    dma = pltpu.SemaphoreType.DMA
    return pl.pallas_call(
        functools.partial(kernel, slots, depth),
        out_shape=pltpu.VMEM((rows, width), BF16),
        in_specs=[pl.BlockSpec(memory_space=pl.ANY)] * 9,
        out_specs=pl.BlockSpec(memory_space=pl.ANY),
        scratch_shapes=[
            pltpu.SMEM(levels.shape, jnp.int32), pltpu.SMEM(lengths.shape, jnp.int32),
            pltpu.SMEM(context.shape, jnp.int32),
            pltpu.VMEM((1, HD), F32), pltpu.VMEM((1, HD), F32), pltpu.VMEM(level_gate.shape, F32),
            row, row, row,
            pltpu.VMEM((heads, CORES, span, HD), BF16),
            pltpu.VMEM((heads, CORES, span, HD), BF16),
            pltpu.VMEM((heads, CORES, span, 2 * HD), BF16),
            pltpu.VMEM((heads, 3, span, HD), BF16),
            pltpu.VMEM((heads, CORES, span, 2 * HD), F32),
            pltpu.VMEM((span, 2 * HD), F32),
            pltpu.VMEM((heads, 3, span, HD), BF16),
            pltpu.VMEM(lines, F32),
            pltpu.VMEM((heads, 3, span, HD), BF16),
            pltpu.VMEM(lines, F32),
            pltpu.VMEM((heads, CORES, span, HD), BF16),
            dma((9,)), dma((3, heads)), dma((3, heads, CORES)), dma((heads, 3, cuts)), dma((heads, 3, cuts)),
            dma((heads, 3, cuts, 2)), dma((heads, 3, cuts, 2)), dma((heads,)), dma((heads,)),
        ],
        compiler_params=pltpu.CompilerParams(
            collective_id=0, has_side_effects=True, vmem_limit_bytes=54 * 2**20
        ),
        cost_estimate=pl.CostEstimate(
            flops=32 * heads * span * span * HD, bytes_accessed=8 * rows * width,
            transcendentals=8 * heads * span * span,
        ),
    )(
        levels, lengths, context, query_gain[None, :], key_gain[None, :], level_gate,
        queries, key_states, value_states,
    )


def shards(
    slots, depth, queries, key_states, value_states, query_gain, key_gain, level_gate, levels, lengths, context
):
    return attention(
        slots, depth, levels, lengths, context, query_gain, key_gain, level_gate,
        queries, key_states, value_states,
    )


def solution(mesh):
    split = P(("slot", "ulysses"), None)
    return jax.shard_map(
        functools.partial(shards, mesh.shape["slot"], mesh.shape["ulysses"]),
        mesh=mesh,
        in_specs=(split, split, split) + (P(),) * 6,
        out_specs=split,
        check_vma=False,
    )
```

```python
import functools
import math

import jax
import jax.numpy as jnp
from jax import lax
from jax.experimental import pallas as pl
from jax.experimental.pallas import tpu as pltpu
from jax.sharding import PartitionSpec as P

HD = 128
CORES = 2
CUTS = 2
MESH = pl.DeviceIdType.MESH
FACTOR = math.log2(math.e) / math.sqrt(HD)
F32, BF16 = jnp.float32, jnp.bfloat16


def kernel(
    slots, depth, levels_hbm, lengths_hbm, context_hbm, query_gain_hbm, key_gain_hbm, gate_hbm,
    q_hbm, k_hbm, v_hbm, out_hbm,
    levels, lengths, context, query_gain, key_gain, gate, q_in, k_in, v_in, q_own, k_own, v_own, q_far, local, ahead, part, part_sum, back, back_sum, done,
    load_sem, in_send, in_recv, q_send, q_recv, part_send, part_recv, out_send, out_recv,
):
    slot, z = lax.axis_index("slot"), lax.axis_index("ulysses")
    chip, core = slot // CORES, slot % CORES
    chips = slots // CORES
    heads = q_own.shape[0]
    span = q_own.shape[2]
    rows = span // depth
    mine = z * CORES + core
    partners = depth * CORES
    cuts = part_sum.shape[2]
    piece = span // cuts

    def chip_at(distance):
        return ((chip + distance + chips) % chips) * CORES + core, z

    def partner(r):
        return chip * CORES + (core + r % CORES) % CORES, (z + r // CORES) % depth

    loads = [
        pltpu.make_async_copy(source, target, load_sem.at[i])
        for i, (source, target) in enumerate((
            (lengths_hbm, lengths), (query_gain_hbm, query_gain), (key_gain_hbm, key_gain),
            (q_hbm, q_in), (k_hbm, k_in), (v_hbm, v_in),
            (context_hbm, context), (levels_hbm, levels), (gate_hbm, gate),
        ))
    ]
    for load in loads:
        load.start()

    barrier = pltpu.get_barrier_semaphore()
    everyone = [partner(r) for r in range(1, partners)] + [chip_at(d) for d in (-1, 1)]
    for other in everyone:
        pl.semaphore_signal(barrier, inc=1, device_id=other, device_id_type=MESH)

    def group(distance):
        return (chip * CORES + distance) % slots

    loads[0].wait()
    for g in range(CORES):
        used = lax.broadcasted_iota(jnp.int32, (span, HD), 0) < lengths[group(g)]
        ones = jnp.where(used, 1.0, 0.0).astype(BF16)
        for j in range(heads):
            v_own[j, g, :, HD:] = ones

    for load in loads[1:]:
        load.wait()
    pl.semaphore_wait(barrier, len(everyone))

    def columns(owner, j):
        return pl.ds(pl.multiple_of((owner * heads + j) * HD, HD), HD)

    own_rows = pl.ds(pl.multiple_of(z * rows, rows), rows)

    def normalize(ref, cols, gain):
        full = ref[:, cols].astype(F32)
        square = jnp.mean(full * full, axis=-1, keepdims=True)
        ref[:, cols] = (full * lax.rsqrt(square + 1e-06) * gain[...]).astype(BF16)

    def clip_values(cols):
        place = lax.broadcasted_iota(jnp.int32, (rows, HD), 0) + z * rows
        v_in[:, cols] = jnp.where(place < lengths[slot], v_in[:, cols].astype(F32), 0.0).astype(BF16)

    def landing(which, j, g):
        if which == 2:
            return v_own.at[j, g, :, pl.ds(0, HD)]
        return (q_own, k_own)[which].at[j, g]

    def send_in(which, j):
        source = (q_in, k_in, v_in)[which]
        if which == 2:
            target = v_own.at[j, core, own_rows, pl.ds(0, HD)]
        else:
            target = (q_own, k_own)[which].at[j, core, own_rows, :]

        def one(r, carry):
            to_slot, to_z = partner(r)
            cols = columns(to_z * CORES + to_slot % CORES, j)
            if which == 0:
                normalize(source, cols, query_gain)
            elif which == 1:
                normalize(source, cols, key_gain)
            else:
                clip_values(cols)

            @pl.when(r == 0)
            def _():
                pltpu.make_async_copy(source.at[:, cols], target, in_recv.at[which, j, core]).start()

            @pl.when(r > 0)
            def _():
                pltpu.make_async_remote_copy(
                    src_ref=source.at[:, cols], dst_ref=target,
                    send_sem=in_send.at[which, j], recv_sem=in_recv.at[which, j, core],
                    device_id=(to_slot, to_z), device_id_type=MESH,
                ).start()

            return carry

        lax.fori_loop(0, partners, one, 0)

    def await_in(which, j, g):
        here = landing(which, j, g)
        pltpu.make_async_copy(here, here, in_recv.at[which, j, g]).wait()

    asks = {0: chip > 0, 1: chip > 0, 2: (chip > 0) & (chip < chips - 1)}
    serves = {0: chip < chips - 1, 1: chip < chips - 1, 2: chip < chips - 2}
    merges = (chip > 0) & (chip < chips - 1)

    def rows_of(h):
        return pl.ds(h * piece, piece)

    def query_copy(j, n, h):
        source = q_far.at[j, 0] if n == 2 else q_own.at[j, n]
        return pltpu.make_async_remote_copy(
            src_ref=source.at[rows_of(h)], dst_ref=q_far.at[j, n, rows_of(h)],
            send_sem=q_send.at[j, n, h], recv_sem=q_recv.at[j, n, h],
            device_id=chip_at(-1), device_id_type=MESH,
        )

    def part_copies(j, n, h):
        return [
            pltpu.make_async_remote_copy(
                src_ref=source, dst_ref=target,
                send_sem=part_send.at[j, n, h, i], recv_sem=part_recv.at[j, n, h, i],
                device_id=chip_at(1), device_id_type=MESH,
            )
            for i, (source, target) in enumerate((
                (part.at[j, n, rows_of(h)], back.at[j, n, rows_of(h)]),
                (part_sum.at[j, n, h], back_sum.at[j, n, h]),
            ))
        ]

    def attend(queries, j, g):
        scores = lax.dot_general(
            queries, k_own[j, g], (((1,), (1,)), ((), ())), preferred_element_type=F32
        )
        weight = jnp.exp2(scores * FACTOR).astype(BF16)
        return jnp.dot(weight, v_own[j, g], preferred_element_type=F32)

    def allowed(distance, offset):
        return jnp.where(context[group(distance)] >= offset, 1.0, 0.0)

    diagonal = lax.broadcasted_iota(jnp.int32, (HD, HD), 0) == lax.broadcasted_iota(jnp.int32, (HD, HD), 1)

    def send_part(j, n, h, both, arrived):
        number = both[:, :HD]
        if arrived is not None:
            number = number + jnp.where(merges, back[j, arrived, rows_of(h), :].astype(F32), 0.0)
        part[j, n, rows_of(h), :] = number.astype(BF16)
        for s in range(piece // HD):
            total = both[s * HD:(s + 1) * HD, HD:]
            total = jnp.sum(jnp.where(diagonal, total, 0.0), axis=0, keepdims=True)
            if arrived is not None:
                total = total + jnp.where(merges, back_sum[j, arrived, h, s:s + 1, :], 0.0)
            part_sum[j, n, h, s:s + 1, :] = total
        for copy in reversed(part_copies(j, n, h)):
            copy.start()

    def query_a_out(j):
        await_in(0, j, 0)

        @pl.when(asks[0])
        def _():
            for h in range(cuts):
                query_copy(j, 0, h).start()

    def query_b_out(j):
        await_in(0, j, 1)

        @pl.when(asks[1])
        def _():
            for h in range(cuts):
                query_copy(j, 1, h).start()

    def query_on(j):
        for h in range(cuts):

            @pl.when(serves[0])
            def _():
                query_copy(j, 0, h).wait_recv()

            @pl.when(asks[2])
            def _():
                query_copy(j, 2, h).start()

    def own_a(j):
        local[j, 0] = attend(q_own[j, 0], j, 0)

    def own_b(j):
        queries = q_own[j, 1]
        local[j, 1] = attend(queries, j, 1) + allowed(1, 1) * attend(queries, j, 0)

    def part_c(j):
        @pl.when(serves[2])
        def _():
            for h in range(cuts):
                query_copy(j, 2, h).wait_recv()
                both = allowed(4, 3) * attend(q_far[j, 2, rows_of(h), :], j, 1)
                send_part(j, 2, h, both, None)

    def part_b(j):
        @pl.when(serves[1])
        def _():
            for h in range(cuts):
                query_copy(j, 1, h).wait_recv()
                queries = q_far[j, 1, rows_of(h), :]
                both = allowed(3, 2) * attend(queries, j, 1) + allowed(3, 3) * attend(queries, j, 0)
                send_part(j, 1, h, both, None)

    def part_a_begin(j):
        @pl.when(serves[0])
        def _():
            queries = q_far[j, 0]
            ahead[...] = allowed(2, 1) * attend(queries, j, 1) + allowed(2, 2) * attend(queries, j, 0)

    def part_a_end(j):
        for h in range(cuts):

            @pl.when(merges)
            def _():
                for copy in part_copies(j, 2, h):
                    copy.wait_recv()

            @pl.when(serves[0])
            def _():
                send_part(j, 0, h, ahead[rows_of(h), :], 2)

    def finish(j, g):
        levels_here = lax.broadcasted_iota(jnp.int32, (gate.shape[0], HD), 0) == levels[group(g)]
        gate_row = jnp.sum(jnp.where(levels_here, gate[:, columns(mine, j)], 0.0), axis=0, keepdims=True)
        target = out_hbm.at[:, columns(mine, j)]
        to_slot = chip * CORES + g
        for h in range(cuts):

            @pl.when(chip > 0)
            def _():
                for copy in part_copies(j, g, h):
                    copy.wait_recv()

            for s in range(piece // HD):
                first = h * piece + s * HD
                here = pl.ds(first, HD)
                both = local[j, g, here, :]
                number = both[:, :HD] + jnp.where(chip > 0, back[j, g, here, :].astype(F32), 0.0)
                total = jnp.where(chip > 0, back_sum[j, g, h, s:s + 1, :], 0.0)
                total = both[:, HD:] + jnp.broadcast_to(total, (HD, HD)).T
                place = lax.broadcasted_iota(jnp.int32, (HD, HD), 0) + first
                attended = jnp.where(place < lengths[group(g)], number / total, 0.0).astype(BF16)
                done[j, g, here, :] = (gate_row * attended.astype(F32)).astype(BF16)
            for to_z in range(h * depth // cuts, (h + 1) * depth // cuts):
                source = done.at[j, g, pl.ds(to_z * rows, rows), :]

                @pl.when((to_slot == slot) & (to_z == z))
                def _():
                    pltpu.make_async_copy(source, target, out_recv.at[j]).start()

                @pl.when((to_slot != slot) | (to_z != z))
                def _():
                    pltpu.make_async_remote_copy(
                        src_ref=source, dst_ref=target, send_sem=out_send.at[j], recv_sem=out_recv.at[j],
                        device_id=(to_slot, to_z), device_id_type=MESH,
                    ).start()

    def keys_in(j, g):
        await_in(1, j, g)
        await_in(2, j, g)

    def heads_in(j):
        @pl.when(core == 0)
        def _():
            for which in (0, 1, 2):
                send_in(which, j)

        @pl.when(core != 0)
        def _():
            for which in (1, 2, 0) if j == 0 else (0, 1, 2):
                send_in(which, j)

    last = heads - 1
    for j in range(heads):
        heads_in(j)
        if j == 0:
            query_a_out(0)
    query_on(0)
    for j in range(last):
        keys_in(j, 1)
        part_c(j)
        if j == 0:
            query_b_out(j)
        keys_in(j, 0)
        part_a_begin(j)
        query_a_out(j + 1)
        own_a(j)
        part_a_end(j)
        part_b(j)
        query_on(j + 1)
        query_b_out(j + 1)
        own_b(j)
    keys_in(last, 1)
    keys_in(last, 0)
    part_a_begin(last)
    for j in range(last - 1):
        finish(j, 0)
        finish(j, 1)
    own_a(last)
    part_c(last)
    finish(last - 1, 0)
    part_a_end(last)
    part_b(last)
    finish(last - 1, 1)
    own_b(last)
    finish(last, 0)
    finish(last, 1)

    sent = q_in.at[:, pl.ds(0, (partners - 1) * HD)]
    got = q_in.at[:, pl.ds(0, partners * HD)]
    for j in range(heads):
        pltpu.make_async_copy(got, got, out_recv.at[j]).wait()
        pltpu.make_async_copy(sent, sent, out_send.at[j]).wait()
        for which in range(3):
            pltpu.make_async_copy(sent, sent, in_send.at[which, j]).wait()
        for n in range(3):
            for h in range(cuts):

                @pl.when(asks[n])
                def _():
                    query_copy(j, n, h).wait_send()

                @pl.when(serves[n])
                def _():
                    for copy in part_copies(j, n, h):
                        copy.wait_send()


def attention(slots, depth, levels, lengths, context, query_gain, key_gain, level_gate, queries, key_states, value_states):
    rows, width = queries.shape
    heads = width // (HD * depth * CORES)
    span = rows * depth
    row = pltpu.VMEM((rows, width), BF16)
    cuts = CUTS
    lines = (heads, 3, cuts, span // cuts // HD, HD)
    dma = pltpu.SemaphoreType.DMA
    return pl.pallas_call(
        functools.partial(kernel, slots, depth),
        out_shape=pltpu.VMEM((rows, width), BF16),
        in_specs=[pl.BlockSpec(memory_space=pl.ANY)] * 9,
        out_specs=pl.BlockSpec(memory_space=pl.ANY),
        scratch_shapes=[
            pltpu.SMEM(levels.shape, jnp.int32), pltpu.SMEM(lengths.shape, jnp.int32),
            pltpu.SMEM(context.shape, jnp.int32),
            pltpu.VMEM((1, HD), F32), pltpu.VMEM((1, HD), F32), pltpu.VMEM(level_gate.shape, F32),
            row, row, row,
            pltpu.VMEM((heads, CORES, span, HD), BF16),
            pltpu.VMEM((heads, CORES, span, HD), BF16),
            pltpu.VMEM((heads, CORES, span, 2 * HD), BF16),
            pltpu.VMEM((heads, 3, span, HD), BF16),
            pltpu.VMEM((heads, CORES, span, 2 * HD), F32),
            pltpu.VMEM((span, 2 * HD), F32),
            pltpu.VMEM((heads, 3, span, HD), BF16),
            pltpu.VMEM(lines, F32),
            pltpu.VMEM((heads, 3, span, HD), BF16),
            pltpu.VMEM(lines, F32),
            pltpu.VMEM((heads, CORES, span, HD), BF16),
            dma((9,)), dma((3, heads)), dma((3, heads, CORES)), dma((heads, 3, cuts)), dma((heads, 3, cuts)),
            dma((heads, 3, cuts, 2)), dma((heads, 3, cuts, 2)), dma((heads,)), dma((heads,)),
        ],
        compiler_params=pltpu.CompilerParams(
            collective_id=0, has_side_effects=True, vmem_limit_bytes=54 * 2**20
        ),
        cost_estimate=pl.CostEstimate(
            flops=32 * heads * span * span * HD, bytes_accessed=8 * rows * width,
            transcendentals=8 * heads * span * span,
        ),
    )(
        levels, lengths, context, query_gain[None, :], key_gain[None, :], level_gate,
        queries, key_states, value_states,
    )


def shards(
    slots, depth, queries, key_states, value_states, query_gain, key_gain, level_gate, levels, lengths, context
):
    return attention(
        slots, depth, levels, lengths, context, query_gain, key_gain, level_gate,
        queries, key_states, value_states,
    )


def solution(mesh):
    split = P(("slot", "ulysses"), None)
    return jax.shard_map(
        functools.partial(shards, mesh.shape["slot"], mesh.shape["ulysses"]),
        mesh=mesh,
        in_specs=(split, split, split) + (P(),) * 6,
        out_specs=split,
        check_vma=False,
    )
```
